256 devices in a mesh: row: 32 (over y, x, core), col: 8 (over z).
Axes of the slice: x: 4, y: 4, z: 8, core: 2. Of those that a mesh axis runs over, the one named last changes fastest.
Arguments:
- tokens: bfloat16 [4096, 4096], P('row', 'col'), may hold values from -6 to 6
- out_grad: bfloat16 [4096, 4096], P('row', 'col'), may hold values from -6 to 6
- weight_in: bfloat16 [4096, 16384], P('col', 'row'), may hold values from -0.09375 to 0.09375
- weight_out: bfloat16 [16384, 4096], P('row', 'col'), may hold values from -0.046875 to 0.046875
Outputs:
- tokens_grad: bfloat16 [4096, 4096], P('row', 'col')
- weight_in_grad: float32 [4096, 16384], P('col', 'row')
- weight_out_grad: float32 [16384, 4096], P('row', 'col')
The draws below stay inside these ranges and needn't reach their ends.
All inputs are finite; a program needn't handle non-finite values.
Results may differ from the reference program's by a relative error of at most 0.029.
Values may be sent and summed in bfloat16 or wider, within the bound.
No kernel may reach another device: no remote copies, remote signals or barrier semaphores. Data moves between devices by JAX's collectives and lax.ppermute only.
A program may use at most 128 MiB of HBM per device.

```python
import math
import jax
import jax.numpy as jnp
from jax import lax

D = 4096
FF = 16384
TOKENS = 4096
N_COL = 8


def shard_levels(rng, extent, cuts, low, top_value):
    level = 1.0
    for dim, blocks in cuts:
        heights = jax.random.uniform(jax.random.fold_in(jax.random.fold_in(rng, 6), dim), (blocks,), jnp.float32, low / len(cuts), top_value / len(cuts))
        level = level * jnp.repeat(jnp.exp(heights), extent[dim] // blocks).reshape((-1,) + (1,) * (len(extent) - 1 - dim))
    return level


def centred(key, dims, scale, limit, split=(), held_as=jnp.bfloat16):
    entries = jax.random.normal(key, dims, jnp.float32) * scale
    if len(split) > 0:
        entries = shard_levels(key, dims, split, -0.22, 0.18) * entries
    return jnp.clip(entries, min=-limit, max=limit).astype(held_as)


def setup_inputs(seed: int = 0) -> dict:
    streams_of = jax.random.split(jax.random.key(seed), 5)
    tokens = centred(streams_of[0], (TOKENS, D), 1.0, 6.0, ((0, 32), (1, 8)))
    out_grad = centred(streams_of[1], (TOKENS, D), 1.0, 6.0, ((0, 32), (1, 8)))
    weight_in = centred(streams_of[2], (D, FF), D ** -0.5, 0.09375, ((0, 8), (1, 32)))
    weight_out = centred(streams_of[3], (FF, D), FF ** -0.5, 0.046875, ((0, 32), (1, 8)))
    return {"tokens": tokens, "out_grad": out_grad, "weight_in": weight_in, "weight_out": weight_out}


cubic_coeff = 0.044715
tanh_scale = math.sqrt(2.0 / math.pi)

def gelu_parts(pre):
    inner = tanh_scale * (pre + cubic_coeff * pre * pre * pre)
    tangent = jnp.tanh(inner)
    gelu_value = 0.5 * pre * (1.0 + tangent)
    derivative = 0.5 * (1.0 + tangent) + 0.5 * pre * (1.0 - tangent * tangent) * tanh_scale * (1.0 + 3.0 * cubic_coeff * pre * pre)
    return (gelu_value, derivative)

def rounded(value):
    low = lax.optimization_barrier(value.astype(jnp.bfloat16))
    return low.astype(jnp.float32)

def reference(tokens, out_grad, weight_in, weight_out):
    block_width = D // N_COL
    pre = jnp.zeros((TOKENS, FF), jnp.float32)
    act_grad = jnp.zeros((TOKENS, FF), jnp.float32)
    for block in range(N_COL):
        first = block * block_width
        last = first + block_width
        pre = pre + rounded(jnp.dot(tokens[:, first:last], weight_in[first:last, :], preferred_element_type=jnp.float32))
        act_grad = act_grad + rounded(jnp.dot(out_grad[:, first:last], weight_out[:, first:last].T, preferred_element_type=jnp.float32))
    gelu_value, derivative = gelu_parts(pre)
    activated = gelu_value.astype(jnp.bfloat16)
    pre_grad = (act_grad * derivative).astype(jnp.bfloat16)
    grad_scale = float(TOKENS) ** (-0.5)
    weight_out_grad = jnp.dot(activated.T, out_grad, preferred_element_type=jnp.float32) * grad_scale
    weight_in_grad = jnp.dot(tokens.T, pre_grad, preferred_element_type=jnp.float32) * grad_scale
    tokens_grad = jnp.dot(pre_grad, weight_in.T, preferred_element_type=jnp.float32).astype(jnp.bfloat16)
    return (tokens_grad, weight_in_grad, weight_out_grad)
```

```python
import math

import jax
import jax.numpy as jnp
from jax import lax
from jax.sharding import PartitionSpec as P

cubic_coeff = 0.044715
tanh_scale = math.sqrt(2.0 / math.pi)

NY, NX, NC, NZ = 4, 4, 2, 8
AXES = ("row", "col")


def gelu_parts(pre):
    inner = tanh_scale * (pre + cubic_coeff * pre * pre * pre)
    tangent = jnp.tanh(inner)
    gelu_value = 0.5 * pre * (1.0 + tangent)
    derivative = 0.5 * (1.0 + tangent) + 0.5 * pre * (1.0 - tangent * tangent) * tanh_scale * (
        1.0 + 3.0 * cubic_coeff * pre * pre
    )
    return (gelu_value, derivative)


def row_of(y, x, core):
    return ((y % NY) * NX + x % NX) * NC + core


def permute(value, target):
    pairs = [
        (row_of(y, x, c) * NZ + z, (lambda t: row_of(*t[:3]) * NZ + t[3] % NZ)(target(y, x, c, z)))
        for y in range(NY)
        for x in range(NX)
        for c in range(NC)
        for z in range(NZ)
    ]
    return lax.ppermute(value, AXES, pairs)


def swap_core(value):
    return permute(value, lambda y, x, c, z: (y, x, 1 - c, z))


def shift_z(value, step):
    return permute(value, lambda y, x, c, z: (y, x, c, z + step))


CHIP_GROUPS = [[row_of(y, x, c) for y in range(NY) for x in range(NX)] for c in range(NC)]


def by_core(core, own, other):
    first = core == 0
    return jnp.where(first, own, other), jnp.where(first, other, own)


def rotate(value, start, count):
    n = value.shape[0]
    copies = -(-(n - 1 + count) // n)
    long = jnp.concatenate([value] * copies, axis=0)
    return lax.dynamic_slice_in_dim(long, start, count, axis=0)


def spread_weight(local):
    up = [local[0:5]]
    down = [local[5:10]]
    for step in range(1, 6):
        up.append(shift_z(up[-1] if step == 1 else up[-1][1:], 1))
        down.append(shift_z(down[-1] if step == 1 else down[-1][:-1], -1))
    blocks = [
        local[7:11],
        down[1][1:5],
        down[2],
        jnp.concatenate([up[5], down[3]], axis=0),
        jnp.concatenate([up[4], down[4]], axis=0),
        jnp.concatenate([up[3], down[5]], axis=0),
        up[2],
        up[1][0:4],
    ]
    n, hidden, feature = blocks[0].shape
    return jnp.concatenate([b.reshape(n * hidden, feature) for b in blocks], axis=1)


def collect_weight_grad(share):
    f32, bf16 = jnp.float32, jnp.bfloat16
    hidden, feature = share.shape[0] // 4, share.shape[1] // NZ
    part = [
        share[:, ((-k) % NZ) * feature : ((-k) % NZ + 1) * feature].reshape(4, hidden, feature)
        for k in range(NZ)
    ]

    def plus(a, b):
        return (a.astype(f32) + b.astype(f32)).astype(bf16)

    cat = lambda *v: jnp.concatenate(v, axis=0)
    low = lambda v: v.astype(bf16)
    up = shift_z(low(part[5][0:1]), -1)
    up = shift_z(cat(low(part[4][0:1]), plus(part[4][1:2], up)), -1)
    up = shift_z(cat(low(part[3][0:1]), plus(part[3][1:3], up)), -1)
    up = shift_z(cat(low(part[2][0:1]), plus(part[2][1:4], up)), -1)
    up = shift_z(cat(low(part[1][0:1]), plus(part[1][1:4], up[0:3]), up[3:4]), -1)
    down = shift_z(low(part[3][3:4]), 1)
    down = shift_z(cat(plus(part[4][2:3], down), low(part[4][3:4])), 1)
    down = shift_z(cat(plus(part[5][1:3], down), low(part[5][3:4])), 1)
    down = shift_z(cat(plus(part[6][0:3], down), low(part[6][3:4])), 1)
    down = shift_z(cat(down[0:1], plus(part[7][0:3], down[1:4]), low(part[7][3:4])), 1)
    up, down, own = up.astype(f32), down.astype(f32), part[0].astype(f32)
    return cat(
        up[0:2] + down[3:5] + own[1:3],
        up[2:3] + own[3:4],
        up[3:5],
        down[0:2],
        down[2:3] + own[0:1],
    )


def dot(a, b, contract):
    return lax.dot_general(a, b, ((contract[:1], contract[1:]), ((), ())), preferred_element_type=jnp.float32)


def per_device(tokens, out_grad, weight_in, weight_out):
    f32, bf16 = jnp.float32, jnp.bfloat16
    core = lax.axis_index("row") % NC
    z = lax.axis_index("col")
    n_tok, n_feat = tokens.shape
    half = n_feat // 2
    n_hid = weight_out.shape[0]
    sub = n_hid // 4

    def halves(value):
        return (
            lax.dynamic_slice_in_dim(value, core * half, half, axis=value.ndim - 1),
            lax.dynamic_slice_in_dim(value, (1 - core) * half, half, axis=value.ndim - 1),
        )

    with jax.named_scope("core_swap_weights"):
        weights = []
        for w in (weight_in.T, weight_out):
            own, other = halves(w)
            low, high = by_core(core, own, swap_core(other))
            both = jnp.concatenate([low, high], axis=0).reshape(NZ, sub, half)
            weights.append(rotate(both, (z + NZ - 2) % NZ, 11))
    with jax.named_scope("core_swap_tokens"):
        own, other = halves(jnp.stack([tokens, out_grad]))
        acts = jnp.stack(by_core(core, own, swap_core(other)), axis=1)
    block = n_tok // 4
    with jax.named_scope("tokens_over_z"):
        acts = acts.reshape(2, NC, 4, block, half).transpose(2, 0, 1, 3, 4)
        acts = lax.all_to_all(jnp.concatenate([acts, acts], axis=0), "col", 0, 0, tiled=True)
        acts = rotate(acts, z, NZ).reshape(NZ, 2, NC * block, half).transpose(1, 2, 0, 3)
        acts = acts.reshape(2, NC * block, NZ * half)
    with jax.named_scope("gather_tokens"):
        tok, grad = (
            lax.all_gather(acts[i], "row", axis=0, tiled=True, axis_index_groups=CHIP_GROUPS) for i in range(2)
        )
    with jax.named_scope("spread_weights"):
        w_in, w_out = (spread_weight(w) for w in weights)

    with jax.named_scope("projections"):
        pre_part = dot(tok, w_in, (1, 1)).astype(bf16)
        act_part = dot(grad, w_out, (1, 1)).astype(bf16)
        pre = pre_part.astype(f32) + swap_core(pre_part).astype(f32)
        act_grad = act_part.astype(f32) + swap_core(act_part).astype(f32)
        gelu_value, derivative = gelu_parts(pre)
        activated = gelu_value.astype(bf16)
        pre_grad = (act_grad * derivative).astype(bf16)

    with jax.named_scope("tokens_grad"):
        n_chip = NY * NX
        share = dot(pre_grad, w_in, (1, 0)).astype(bf16).reshape(n_chip, NC * block, NZ * half)
        share = lax.all_to_all(share, "row", 0, 0, tiled=True, axis_index_groups=CHIP_GROUPS)
        share = jnp.sum(share.astype(f32), axis=0).astype(bf16)
        share = share.reshape(NC * block, NZ, half).transpose(1, 0, 2)
        share = rotate(share, (NZ - z) % NZ, NZ)
        share = lax.all_to_all(share, "col", 0, 0, tiled=True).astype(f32)
        share = (share[0:4] + share[4:8]).reshape(4, NC, block, half).transpose(1, 0, 2, 3)
        share = share.reshape(NC, n_tok, half)
        own = lax.dynamic_index_in_dim(share, core, axis=0, keepdims=False).astype(bf16)
        other = lax.dynamic_index_in_dim(share, 1 - core, axis=0, keepdims=False).astype(bf16)
        tokens_grad = jnp.concatenate(by_core(core, own, swap_core(other)), axis=1)

    with jax.named_scope("weight_grads"):
        grad_scale = float(n_tok * NY * NX * NC) ** (-0.5)
        grads = []
        for hid, feat in ((activated, grad), (pre_grad, tok)):
            total = collect_weight_grad(dot(hid, feat, (0, 0)))
            total = rotate(total, (2 + NZ - z) % NZ, NZ).reshape(NC, n_hid, half)
            own = lax.dynamic_index_in_dim(total, core, axis=0, keepdims=False)
            other = lax.dynamic_index_in_dim(total, 1 - core, axis=0, keepdims=False)
            other = swap_core(other.astype(bf16)).astype(f32)
            grads.append(jnp.concatenate(by_core(core, own, other), axis=1) * grad_scale)
        weight_out_grad, weight_in_grad = grads[0], grads[1].T
    return (tokens_grad, weight_in_grad, weight_out_grad)


def solution(mesh):
    in_specs = (P("row", "col"), P("row", "col"), P("col", "row"), P("row", "col"))
    out_specs = (P("row", "col"), P("col", "row"), P("row", "col"))
    return jax.shard_map(
        per_device, mesh=mesh, in_specs=in_specs, out_specs=out_specs, check_vma=False
    )
```

```python
import math

import jax
import jax.numpy as jnp
from jax import lax
from jax.experimental import pallas as pl
from jax.experimental.pallas import tpu as pltpu
from jax.sharding import PartitionSpec as P

cubic_coeff = 0.044715
tanh_scale = math.sqrt(2.0 / math.pi)

NY, NX, NC, NZ = 4, 4, 2, 8
AXES = ("row", "col")


def gelu_parts(pre):
    inner = tanh_scale * (pre + cubic_coeff * pre * pre * pre)
    tangent = jnp.tanh(inner)
    gelu_value = 0.5 * pre * (1.0 + tangent)
    derivative = 0.5 * (1.0 + tangent) + 0.5 * pre * (1.0 - tangent * tangent) * tanh_scale * (
        1.0 + 3.0 * cubic_coeff * pre * pre
    )
    return (gelu_value, derivative)


def row_of(y, x, core):
    return ((y % NY) * NX + x % NX) * NC + core


def permute(value, target):
    pairs = [
        (row_of(y, x, c) * NZ + z, (lambda t: row_of(*t[:3]) * NZ + t[3] % NZ)(target(y, x, c, z)))
        for y in range(NY)
        for x in range(NX)
        for c in range(NC)
        for z in range(NZ)
    ]
    return lax.ppermute(value, AXES, pairs)


def swap_core(value):
    return permute(value, lambda y, x, c, z: (y, x, 1 - c, z))


def shift_z(value, step):
    return permute(value, lambda y, x, c, z: (y, x, c, z + step))


CHIP_GROUPS = [[row_of(y, x, c) for y in range(NY) for x in range(NX)] for c in range(NC)]


def by_core(core, own, other):
    first = core == 0
    return jnp.where(first, own, other), jnp.where(first, other, own)


def rotate(value, start, count):
    n = value.shape[0]
    copies = -(-(n - 1 + count) // n)
    long = jnp.concatenate([value] * copies, axis=0)
    return lax.dynamic_slice_in_dim(long, start, count, axis=0)


def cat(*values):
    return jnp.concatenate(values, axis=0)


def spread_first(local):
    return shift_z(local[2:5], 1), shift_z(local[5:8], -1)


def spread_rest(local, first):
    ups, downs = [first[0]], [first[1]]
    for step in range(2, 6):
        ups[-1], downs[-1] = yield ups[-1], downs[-1]
        up, down = ups[-1], downs[-1]
        if step == 4:
            up, down = cat(up[1:3], local[1:2]), cat(down[0:2], local[8:9])
        elif step == 5:
            up, down = cat(up[1:3], local[0:1]), cat(down[0:1], down[2:3], local[9:10])
        ups.append(shift_z(up, 1))
        downs.append(shift_z(down, -1))
    u1, u2, u3, u4, u5 = ups
    d1, d2, d3, d4, d5 = downs
    blocks = [
        (local[7:11],),
        (d1[1:3], d4[2:3], d5[2:3]),
        (d2, d5[1:2]),
        (u5[0:1], d3),
        (u4[0:2], d4[0:2]),
        (u3, d5[0:1]),
        (u5[1:2], u2),
        (u5[2:3], u4[2:3], u1[0:2]),
    ]
    hidden, feature = local.shape[2:]
    yield [
        jnp.concatenate([cat(*(p[:, i] for p in block)).reshape(4 * hidden, feature) for block in blocks], axis=1)
        for i in range(2)
    ]


def pad(value, before, after):
    return jnp.pad(value.astype(jnp.float32), ((before, after), (0, 0), (0, 0)))


def plus(a, b):
    return a.astype(jnp.float32) + b.astype(jnp.float32)


def weight_grad_steps(share, first_up, first_down):
    bf16 = jnp.bfloat16
    share = share.reshape(NZ, 4, share.shape[1] // 4, share.shape[2])
    part = [share[-k % NZ] for k in range(NZ)]
    send = lambda up, down: (shift_z(up.astype(bf16), -1), shift_z(down.astype(bf16), 1))
    up1, down1 = yield send(first_up, first_down)
    up2, down2 = yield send(
        pad(part[4][0:2], 0, 1) + pad(part[1][1:2], 2, 0) + pad(up1[0:2], 1, 0),
        pad(part[4][2:4], 0, 1) + pad(part[7][2:3], 2, 0) + pad(down1[0:1], 0, 2) + pad(down1[1:2], 2, 0),
    )
    up, down = yield send(part[3][0:3] + pad(up2[0:2], 1, 0), part[5][1:4] + pad(down2[0:2], 0, 1))
    up, down = yield send(plus(part[2][1:4], up), plus(part[6][0:3], down))
    up, down = send(pad(part[1][2:4], 0, 1) + pad(up, 0, 0), pad(part[7][0:2], 1, 0) + pad(down, 0, 0))
    own = part[0]
    yield (
        pad(up, 2, 3) + pad(up1[2:3], 0, 7) + pad(up2[2:3], 1, 6)
        + pad(down, 5, 0) + pad(down2[2:3], 0, 7) + pad(down1[2:3], 1, 6)
        + pad(own[0:1], 7, 0) + pad(own[1:4], 0, 5)
    ).astype(bf16)


def call_options(rows, depth, columns):
    size = rows * depth + depth * columns + rows * columns
    return dict(
        compiler_params=pltpu.CompilerParams(vmem_limit_bytes=32 * 2**20),
        cost_estimate=pl.CostEstimate(
            flops=2 * rows * depth * columns, bytes_accessed=2 * size, transcendentals=0
        ),
    )


def project_kernel(x_ref, weight_ref, out_ref):
    total = lax.dot_general(
        x_ref[...], weight_ref[...], (((1,), (1,)), ((), ())), preferred_element_type=jnp.float32
    )
    out_ref[...] = total.astype(out_ref.dtype)


def project(x, part, weight):
    rows, (hidden, features) = x.shape[0], weight.shape
    tile = rows // 4
    return pl.pallas_call(
        project_kernel,
        grid=(4,),
        in_specs=[
            pl.BlockSpec((tile, features), lambda i: (i, part)),
            pl.BlockSpec((hidden, features), lambda i: (0, 0)),
        ],
        out_specs=pl.BlockSpec((tile, hidden), lambda i: (i, 0)),
        out_shape=jax.ShapeDtypeStruct((rows, hidden), jnp.bfloat16),
        **call_options(rows, features, hidden),
    )(x, weight)


def unproject_kernel(grad_ref, weight_ref, out_ref):
    total = jnp.dot(grad_ref[...], weight_ref[...], preferred_element_type=jnp.float32)
    out_ref[...] = total.astype(out_ref.dtype)


def unproject(grad, weight):
    rows, (hidden, features) = grad.shape[0], weight.shape
    tile = rows // 4
    return pl.pallas_call(
        unproject_kernel,
        grid=(4,),
        in_specs=[
            pl.BlockSpec((tile, hidden), lambda i: (i, 0)),
            pl.BlockSpec((hidden, features), lambda i: (0, 0)),
        ],
        out_specs=pl.BlockSpec((tile, features), lambda i: (i, 0)),
        out_shape=jax.ShapeDtypeStruct((rows, features), jnp.bfloat16),
        **call_options(rows, hidden, features),
    )(grad, weight)


FIRST_UP = (3, 6, 7)
FIRST_DOWN = (5, 2, 1)


def share_kernel(hid_ref, feat_ref, out_ref, up_ref, down_ref, turned_ref):
    i = pl.program_id(0)

    @pl.when(i == 0)
    def _():
        turned_ref[...] = hid_ref[...].T

    total = jnp.dot(turned_ref[...], feat_ref[...], preferred_element_type=jnp.float32)
    total = total.astype(out_ref.dtype)
    out_ref[0] = total
    subset = total.shape[0] // 4
    for at in range(3):

        @pl.when(i == FIRST_UP[at])
        def _():
            up_ref[at] = total[:subset]

        @pl.when(i == FIRST_DOWN[at])
        def _():
            down_ref[at] = total[3 * subset :]


def weight_share(hid, feat, part):
    rows, hidden = hid.shape
    width = feat.shape[1] // (2 * NZ)
    first = pl.BlockSpec((3, hidden // 4, width), lambda i: (0, 0, 0))
    return pl.pallas_call(
        share_kernel,
        grid=(NZ,),
        in_specs=[
            pl.BlockSpec((rows, hidden), lambda i: (0, 0)),
            pl.BlockSpec((rows, width), lambda i: (0, part * NZ + i)),
        ],
        out_specs=[pl.BlockSpec((1, hidden, width), lambda i: (i, 0, 0)), first, first],
        out_shape=[
            jax.ShapeDtypeStruct(shape, jnp.bfloat16)
            for shape in [(NZ, hidden, width)] + [(3, hidden // 4, width)] * 2
        ],
        scratch_shapes=[pltpu.VMEM((hidden, rows), jnp.bfloat16)],
        **call_options(hidden, rows, NZ * width),
    )(hid, feat)


def per_device(tokens, out_grad, weight_in, weight_out):
    f32, bf16 = jnp.float32, jnp.bfloat16
    core = lax.axis_index("row") % NC
    z = lax.axis_index("col")
    n_tok, n_feat = tokens.shape
    half = n_feat // 2
    n_hid = weight_out.shape[0]
    sub = n_hid // 4

    def halves(value):
        return (
            lax.dynamic_slice_in_dim(value, core * half, half, axis=value.ndim - 1),
            lax.dynamic_slice_in_dim(value, (1 - core) * half, half, axis=value.ndim - 1),
        )

    with jax.named_scope("core_swap"):
        own, other = halves(jnp.stack([out_grad, tokens]))
        acts = jnp.stack(by_core(core, own, swap_core(other)), axis=1)
        own, other = halves(jnp.stack([weight_in.T, weight_out]))
        low, high = by_core(core, own, swap_core(other))
        weights = jnp.concatenate([low.reshape(2, 4, sub, half), high.reshape(2, 4, sub, half)], axis=1)
        weights = rotate(weights.transpose(1, 0, 2, 3), (z + NZ - 2) % NZ, 11)
        acts, weights = lax.optimization_barrier((acts, weights))
    block = n_tok // 4
    with jax.named_scope("tokens_over_z"):
        acts = acts.reshape(2, NC, 4, block, half).transpose(2, 0, 1, 3, 4)
        acts = lax.all_to_all(jnp.concatenate([acts, acts], axis=0), "col", 0, 0, tiled=True)
        acts = rotate(acts, z, NZ).reshape(NZ, 2, NC * block, half).transpose(1, 2, 0, 3)
        acts = acts.reshape(2, NC * block, NZ * half)
    with jax.named_scope("gather_tokens"):
        width = NZ * half
        acts = lax.all_gather(
            jnp.concatenate([acts[0], acts[1]], axis=1), "row", axis=0, tiled=True, axis_index_groups=CHIP_GROUPS
        )
    with jax.named_scope("spread_weights"):
        spread = spread_rest(weights, spread_first(weights))
        ring = next(spread)
        for step in range(3):
            ring = spread.send(lax.optimization_barrier(ring))
        w_in, w_out = spread.send(lax.optimization_barrier(ring))

    with jax.named_scope("projections"):
        pre_part = project(acts, 1, w_in)
        pre = pre_part.astype(f32) + swap_core(pre_part).astype(f32)
        act_part = project(acts, 0, w_out)
        act_grad = act_part.astype(f32) + swap_core(act_part).astype(f32)
        gelu_value, derivative = gelu_parts(pre)
        activated = gelu_value.astype(bf16)
    with jax.named_scope("weight_grads"):
        shares = weight_share(activated, acts, 0)
        shares, act_grad = lax.optimization_barrier((shares, act_grad))
        chains = [weight_grad_steps(*shares)]
        moving = [next(chains[0])]
    with jax.named_scope("projections"):
        pre_grad = (act_grad * derivative).astype(bf16)
    with jax.named_scope("tokens_grad_sum"):
        share = unproject(pre_grad, w_in).reshape(NY * NX, NC * block, width)
        pre_grad, share = lax.optimization_barrier((pre_grad, share))
        share = lax.all_to_all(share, "row", 0, 0, tiled=True, axis_index_groups=CHIP_GROUPS)

    with jax.named_scope("weight_grads"):
        pre_grad, moving[0] = lax.optimization_barrier((pre_grad, moving[0]))
        chains.append(weight_grad_steps(*weight_share(pre_grad, acts, 1)))
        moving.append(next(chains[1]))
        for step in range(2, 5):
            moving = [c.send(m) for c, m in zip(chains, moving)]
        totals = [c.send(m) for c, m in zip(chains, moving)]

    with jax.named_scope("tokens_grad_sum"):
        share = jnp.sum(share.astype(f32), axis=0).astype(bf16)
        share = share.reshape(NC * block, NZ, half).transpose(1, 0, 2)
        share = rotate(share, (NZ - z) % NZ, NZ)
        share, totals = lax.optimization_barrier((share, totals))

    with jax.named_scope("tokens_grad_home"):
        share = lax.all_to_all(share, "col", 0, 0, tiled=True).astype(f32)
        share = (share[0:4] + share[4:8]).reshape(4, NC, block, half).transpose(1, 0, 2, 3)
        share = share.reshape(NC, n_tok, half).astype(bf16)
        own = lax.dynamic_index_in_dim(share, core, axis=0, keepdims=False)
        other = lax.dynamic_index_in_dim(share, 1 - core, axis=0, keepdims=False)
        tokens_grad = jnp.concatenate(by_core(core, own, swap_core(other)), axis=1)

    with jax.named_scope("weight_grads_home"):
        grad_scale = float(n_tok * NY * NX * NC) ** (-0.5)
        grads = []
        for total in totals:
            total = jnp.concatenate([total, total[0:3]], axis=0)
            own, other = (
                lax.dynamic_slice_in_dim(total, (2 + NZ - z + 4 * c) % NZ, 4, axis=0).reshape(n_hid, half)
                for c in (core, 1 - core)
            )
            low, high = by_core(core, own, swap_core(other))
            grads.append(jnp.concatenate([low, high], axis=1).astype(f32) * grad_scale)
        weight_out_grad, weight_in_grad = grads[0], grads[1].T
    return (tokens_grad, weight_in_grad, weight_out_grad)


def solution(mesh):
    in_specs = (P("row", "col"), P("row", "col"), P("col", "row"), P("row", "col"))
    out_specs = (P("row", "col"), P("col", "row"), P("row", "col"))
    return jax.shard_map(
        per_device, mesh=mesh, in_specs=in_specs, out_specs=out_specs, check_vma=False
    )
```

```python
import math

import jax
import jax.numpy as jnp
from jax import lax
from jax.experimental import pallas as pl
from jax.experimental.pallas import tpu as pltpu
from jax.sharding import PartitionSpec as P

cubic_coeff = 0.044715
tanh_scale = math.sqrt(2.0 / math.pi)

NY, NX, NC, NZ = 4, 4, 2, 8
AXES = ("row", "col")


def gelu_parts(pre):
    inner = tanh_scale * (pre + cubic_coeff * pre * pre * pre)
    tangent = jnp.tanh(inner)
    gelu_value = 0.5 * pre * (1.0 + tangent)
    derivative = 0.5 * (1.0 + tangent) + 0.5 * pre * (1.0 - tangent * tangent) * tanh_scale * (
        1.0 + 3.0 * cubic_coeff * pre * pre
    )
    return (gelu_value, derivative)


def row_of(y, x, core):
    return ((y % NY) * NX + x % NX) * NC + core


def permute(value, target):
    pairs = [
        (row_of(y, x, c) * NZ + z, (lambda t: row_of(*t[:3]) * NZ + t[3] % NZ)(target(y, x, c, z)))
        for y in range(NY)
        for x in range(NX)
        for c in range(NC)
        for z in range(NZ)
    ]
    return lax.ppermute(value, AXES, pairs)


def swap_core(value):
    return permute(value, lambda y, x, c, z: (y, x, 1 - c, z))


def shift_z(value, step):
    return permute(value, lambda y, x, c, z: (y, x, c, z + step))


CHIP_GROUPS = [[row_of(y, x, c) for y in range(NY) for x in range(NX)] for c in range(NC)]


def by_core(core, own, other):
    first = core == 0
    return jnp.where(first, own, other), jnp.where(first, other, own)


def rotate(value, start, count):
    n = value.shape[0]
    copies = -(-(n - 1 + count) // n)
    long = jnp.concatenate([value] * copies, axis=0)
    return lax.dynamic_slice_in_dim(long, start, count, axis=0)


def cat(*values):
    return jnp.concatenate(values, axis=0)


def spread_first(local):
    return shift_z(local[2:5], 1), shift_z(local[5:8], -1)


def spread_rest(local, first):
    ups, downs = [first[0]], [first[1]]
    for step in range(2, 6):
        ups[-1], downs[-1] = yield ups[-1], downs[-1]
        up, down = ups[-1], downs[-1]
        if step == 4:
            up, down = cat(up[1:3], local[1:2]), cat(down[0:2], local[8:9])
        elif step == 5:
            up, down = cat(up[1:3], local[0:1]), cat(down[0:1], down[2:3], local[9:10])
        ups.append(shift_z(up, 1))
        downs.append(shift_z(down, -1))
    u1, u2, u3, u4, u5 = ups
    d1, d2, d3, d4, d5 = downs
    blocks = [
        (local[7:11],),
        (d1[1:3], d4[2:3], d5[2:3]),
        (d2, d5[1:2]),
        (u5[0:1], d3),
        (u4[0:2], d4[0:2]),
        (u3, d5[0:1]),
        (u5[1:2], u2),
        (u5[2:3], u4[2:3], u1[0:2]),
    ]
    hidden, feature = local.shape[2:]
    yield [
        jnp.concatenate([cat(*(p[:, i] for p in block)).reshape(4 * hidden, feature) for block in blocks], axis=1)
        for i in range(2)
    ]


def pad(value, before, after):
    return jnp.pad(value.astype(jnp.float32), ((before, after), (0, 0), (0, 0)))


def plus(a, b):
    return a.astype(jnp.float32) + b.astype(jnp.float32)


def weight_grad_steps(share, first_up, first_down):
    bf16 = jnp.bfloat16
    share = share.reshape(NZ, 4, share.shape[1] // 4, share.shape[2])
    part = [share[-k % NZ] for k in range(NZ)]
    send = lambda up, down: (shift_z(up.astype(bf16), -1), shift_z(down.astype(bf16), 1))
    up1, down1 = yield send(first_up, first_down)
    up2, down2 = yield send(
        pad(part[4][0:2], 0, 1) + pad(part[1][1:2], 2, 0) + pad(up1[0:2], 1, 0),
        pad(part[4][2:4], 0, 1) + pad(part[7][2:3], 2, 0) + pad(down1[0:1], 0, 2) + pad(down1[1:2], 2, 0),
    )
    up, down = yield send(part[3][0:3] + pad(up2[0:2], 1, 0), part[5][1:4] + pad(down2[0:2], 0, 1))
    up, down = yield send(plus(part[2][1:4], up), plus(part[6][0:3], down))
    up, down = send(pad(part[1][2:4], 0, 1) + pad(up, 0, 0), pad(part[7][0:2], 1, 0) + pad(down, 0, 0))
    own = part[0]
    yield (
        pad(up, 2, 3) + pad(up1[2:3], 0, 7) + pad(up2[2:3], 1, 6)
        + pad(down, 5, 0) + pad(down2[2:3], 0, 7) + pad(down1[2:3], 1, 6)
        + pad(own[0:1], 7, 0) + pad(own[1:4], 0, 5)
    ).astype(bf16)


def call_options(rows, depth, columns):
    size = rows * depth + depth * columns + rows * columns
    return dict(
        compiler_params=pltpu.CompilerParams(vmem_limit_bytes=32 * 2**20),
        cost_estimate=pl.CostEstimate(
            flops=2 * rows * depth * columns, bytes_accessed=2 * size, transcendentals=0
        ),
    )


def project_kernel(x_ref, weight_ref, out_ref):
    total = lax.dot_general(
        x_ref[...], weight_ref[...], (((1,), (1,)), ((), ())), preferred_element_type=jnp.float32
    )
    out_ref[...] = total.astype(out_ref.dtype)


def project(x, part, weight):
    rows, (hidden, features) = x.shape[0], weight.shape
    tile = rows // 4
    return pl.pallas_call(
        project_kernel,
        grid=(4,),
        in_specs=[
            pl.BlockSpec((tile, features), lambda i: (i, part)),
            pl.BlockSpec((hidden, features), lambda i: (0, 0)),
        ],
        out_specs=pl.BlockSpec((tile, hidden), lambda i: (i, 0)),
        out_shape=jax.ShapeDtypeStruct((rows, hidden), jnp.bfloat16),
        **call_options(rows, features, hidden),
    )(x, weight)


def unproject_kernel(grad_ref, weight_ref, out_ref):
    total = jnp.dot(grad_ref[...], weight_ref[...], preferred_element_type=jnp.float32)
    out_ref[...] = total.astype(out_ref.dtype)


def unproject(grad, weight):
    rows, (hidden, features) = grad.shape[0], weight.shape
    tile = rows // 4
    return pl.pallas_call(
        unproject_kernel,
        grid=(4,),
        in_specs=[
            pl.BlockSpec((tile, hidden), lambda i: (i, 0)),
            pl.BlockSpec((hidden, features), lambda i: (0, 0)),
        ],
        out_specs=pl.BlockSpec((tile, features), lambda i: (i, 0)),
        out_shape=jax.ShapeDtypeStruct((rows, features), jnp.bfloat16),
        **call_options(rows, hidden, features),
    )(grad, weight)


FIRST_UP = (3, 6, 7)
FIRST_DOWN = (5, 2, 1)


def share_kernel(hid_ref, feat_ref, out_ref, up_ref, down_ref, turned_ref):
    i = pl.program_id(0)

    @pl.when(i == 0)
    def _():
        turned_ref[...] = hid_ref[...].T

    total = jnp.dot(turned_ref[...], feat_ref[...], preferred_element_type=jnp.float32)
    total = total.astype(out_ref.dtype)
    out_ref[0] = total
    subset = total.shape[0] // 4
    for at in range(3):

        @pl.when(i == FIRST_UP[at])
        def _():
            up_ref[at] = total[:subset]

        @pl.when(i == FIRST_DOWN[at])
        def _():
            down_ref[at] = total[3 * subset :]


def weight_share(hid, feat, part):
    rows, hidden = hid.shape
    width = feat.shape[1] // (2 * NZ)
    first = pl.BlockSpec((3, hidden // 4, width), lambda i: (0, 0, 0))
    return pl.pallas_call(
        share_kernel,
        grid=(NZ,),
        in_specs=[
            pl.BlockSpec((rows, hidden), lambda i: (0, 0)),
            pl.BlockSpec((rows, width), lambda i: (0, part * NZ + i)),
        ],
        out_specs=[pl.BlockSpec((1, hidden, width), lambda i: (i, 0, 0)), first, first],
        out_shape=[
            jax.ShapeDtypeStruct(shape, jnp.bfloat16)
            for shape in [(NZ, hidden, width)] + [(3, hidden // 4, width)] * 2
        ],
        scratch_shapes=[pltpu.VMEM((hidden, rows), jnp.bfloat16)],
        **call_options(hidden, rows, NZ * width),
    )(hid, feat)


def per_device(tokens, out_grad, weight_in, weight_out):
    f32, bf16 = jnp.float32, jnp.bfloat16
    core = lax.axis_index("row") % NC
    z = lax.axis_index("col")
    n_tok, n_feat = tokens.shape
    half = n_feat // 2
    n_hid = weight_out.shape[0]
    sub = n_hid // 4

    def halves(value):
        return (
            lax.dynamic_slice_in_dim(value, core * half, half, axis=value.ndim - 1),
            lax.dynamic_slice_in_dim(value, (1 - core) * half, half, axis=value.ndim - 1),
        )

    with jax.named_scope("core_swap"):
        own, other = halves(jnp.stack([out_grad, tokens]))
        acts = jnp.stack(by_core(core, own, swap_core(other)), axis=1)
        acts, weight_in, weight_out = lax.optimization_barrier((acts, weight_in, weight_out))
        own, other = halves(jnp.stack([weight_in.T, weight_out]))
        low, high = by_core(core, own, swap_core(other))
        weights = jnp.concatenate([low.reshape(2, 4, sub, half), high.reshape(2, 4, sub, half)], axis=1)
        weights = rotate(weights.transpose(1, 0, 2, 3), (z + NZ - 2) % NZ, 11)
    block = n_tok // 4
    with jax.named_scope("tokens_over_z"):
        acts = acts.reshape(2, NC, 4, block, half).transpose(2, 0, 1, 3, 4)
        acts = lax.all_to_all(jnp.concatenate([acts, acts], axis=0), "col", 0, 0, tiled=True)
        acts = rotate(acts, z, NZ).reshape(NZ, 2, NC * block, half).transpose(1, 2, 0, 3)
        acts = acts.reshape(2, NC * block, NZ * half)
    with jax.named_scope("gather_tokens"):
        width = NZ * half
        acts = lax.all_gather(
            jnp.concatenate([acts[0], acts[1]], axis=1), "row", axis=0, tiled=True, axis_index_groups=CHIP_GROUPS
        )
    with jax.named_scope("spread_weights"):
        spread = spread_rest(weights, spread_first(weights))
        ring = next(spread)
        for step in range(3):
            ring = spread.send(lax.optimization_barrier(ring))
        w_in, w_out = spread.send(lax.optimization_barrier(ring))

    with jax.named_scope("projections"):
        pre_part = project(acts, 1, w_in)
        pre = pre_part.astype(f32) + swap_core(pre_part).astype(f32)
        act_part = project(acts, 0, w_out)
        act_grad = act_part.astype(f32) + swap_core(act_part).astype(f32)
        gelu_value, derivative = gelu_parts(pre)
        activated, pre_grad = lax.optimization_barrier(
            (gelu_value.astype(bf16), (act_grad * derivative).astype(bf16))
        )
    with jax.named_scope("tokens_grad_sum"):
        share = unproject(pre_grad, w_in).reshape(NY * NX, NC * block, width)
        share, activated, pre_grad = lax.optimization_barrier((share, activated, pre_grad))
        share = lax.all_to_all(share, "row", 0, 0, tiled=True, axis_index_groups=CHIP_GROUPS)
    with jax.named_scope("weight_grads"):
        chains = [
            weight_grad_steps(*weight_share(activated, acts, 0)),
            weight_grad_steps(*weight_share(pre_grad, acts, 1)),
        ]
        moving = [next(c) for c in chains]
        for step in range(3):
            moving = [c.send(m) for c, m in zip(chains, moving)]
    with jax.named_scope("tokens_grad_sum"):
        share = jnp.sum(share.astype(f32), axis=0).astype(bf16)
        share = share.reshape(NC * block, NZ, half).transpose(1, 0, 2)
        share = rotate(share, (NZ - z) % NZ, NZ)
        share, moving[1] = lax.optimization_barrier((share, moving[1]))
        totals = [c.send(m) for c, m in zip(chains, moving)]

    with jax.named_scope("tokens_grad_home"):
        share = lax.all_to_all(share, "col", 0, 0, tiled=True).astype(f32)
        share = (share[0:4] + share[4:8]).reshape(4, NC, block, half).transpose(1, 0, 2, 3)
        share = share.reshape(NC, n_tok, half).astype(bf16)
        own = lax.dynamic_index_in_dim(share, core, axis=0, keepdims=False)
        other = lax.dynamic_index_in_dim(share, 1 - core, axis=0, keepdims=False)
        tokens_grad = jnp.concatenate(by_core(core, own, swap_core(other)), axis=1)

    with jax.named_scope("weight_grads_home"):
        grad_scale = float(n_tok * NY * NX * NC) ** (-0.5)
        grads = []
        for total in totals:
            total = jnp.concatenate([total, total[0:3]], axis=0)
            own, other = (
                lax.dynamic_slice_in_dim(total, (2 + NZ - z + 4 * c) % NZ, 4, axis=0).reshape(n_hid, half)
                for c in (core, 1 - core)
            )
            low, high = by_core(core, own, swap_core(other))
            grads.append(jnp.concatenate([low, high], axis=1).astype(f32) * grad_scale)
        weight_out_grad, weight_in_grad = grads[0], grads[1].T
    return (tokens_grad, weight_in_grad, weight_out_grad)


def solution(mesh):
    in_specs = (P("row", "col"), P("row", "col"), P("col", "row"), P("row", "col"))
    out_specs = (P("row", "col"), P("col", "row"), P("row", "col"))
    return jax.shard_map(
        per_device, mesh=mesh, in_specs=in_specs, out_specs=out_specs, check_vma=False
    )
```

```python
import math

import jax
import jax.numpy as jnp
from jax import lax
from jax.experimental import pallas as pl
from jax.experimental.pallas import tpu as pltpu
from jax.sharding import PartitionSpec as P

cubic_coeff = 0.044715
tanh_scale = math.sqrt(2.0 / math.pi)

NY, NX, NC, NZ = 4, 4, 2, 8
AXES = ("row", "col")


def gelu_parts(pre):
    inner = tanh_scale * (pre + cubic_coeff * pre * pre * pre)
    tangent = jnp.tanh(inner)
    gelu_value = 0.5 * pre * (1.0 + tangent)
    derivative = 0.5 * (1.0 + tangent) + 0.5 * pre * (1.0 - tangent * tangent) * tanh_scale * (
        1.0 + 3.0 * cubic_coeff * pre * pre
    )
    return (gelu_value, derivative)


def row_of(y, x, core):
    return ((y % NY) * NX + x % NX) * NC + core


def permute(value, target):
    pairs = [
        (row_of(y, x, c) * NZ + z, (lambda t: row_of(*t[:3]) * NZ + t[3] % NZ)(target(y, x, c, z)))
        for y in range(NY)
        for x in range(NX)
        for c in range(NC)
        for z in range(NZ)
    ]
    return lax.ppermute(value, AXES, pairs)


def swap_core(value):
    return permute(value, lambda y, x, c, z: (y, x, 1 - c, z))


def shift_z(value, step):
    return permute(value, lambda y, x, c, z: (y, x, c, z + step))


CHIP_GROUPS = [[row_of(y, x, c) for y in range(NY) for x in range(NX)] for c in range(NC)]


def by_core(core, own, other):
    first = core == 0
    return jnp.where(first, own, other), jnp.where(first, other, own)


def rotate(value, start, count):
    n = value.shape[0]
    copies = -(-(n - 1 + count) // n)
    long = jnp.concatenate([value] * copies, axis=0)
    return lax.dynamic_slice_in_dim(long, start, count, axis=0)


def cat(*values):
    return jnp.concatenate(values, axis=0)


def spread_first(local):
    return shift_z(local[2:5], 1), shift_z(local[5:8], -1)


def spread_rest(local, first):
    ups, downs = [first[0]], [first[1]]
    for step in range(2, 6):
        ups[-1], downs[-1] = yield ups[-1], downs[-1]
        up, down = ups[-1], downs[-1]
        if step == 4:
            up, down = cat(up[1:3], local[1:2]), cat(down[0:2], local[8:9])
        elif step == 5:
            up, down = cat(up[1:3], local[0:1]), cat(down[0:1], down[2:3], local[9:10])
        ups.append(shift_z(up, 1))
        downs.append(shift_z(down, -1))
    u1, u2, u3, u4, u5 = ups
    d1, d2, d3, d4, d5 = downs
    blocks = [
        (local[7:11],),
        (d1[1:3], d4[2:3], d5[2:3]),
        (d2, d5[1:2]),
        (u5[0:1], d3),
        (u4[0:2], d4[0:2]),
        (u3, d5[0:1]),
        (u5[1:2], u2),
        (u5[2:3], u4[2:3], u1[0:2]),
    ]
    hidden, feature = local.shape[2:]
    yield [
        jnp.concatenate([cat(*(p[:, i] for p in block)).reshape(4 * hidden, feature) for block in blocks], axis=1)
        for i in range(2)
    ]


def pad(value, before, after):
    return jnp.pad(value.astype(jnp.float32), ((before, after), (0, 0), (0, 0)))


def plus(a, b):
    return a.astype(jnp.float32) + b.astype(jnp.float32)


def weight_grad_steps(share, first_up, first_down):
    bf16 = jnp.bfloat16
    share = share.reshape(NZ, 4, share.shape[1] // 4, share.shape[2])
    part = [share[-k % NZ] for k in range(NZ)]
    send = lambda up, down: (shift_z(up.astype(bf16), -1), shift_z(down.astype(bf16), 1))
    up1, down1 = yield send(first_up, first_down)
    up2, down2 = yield send(
        pad(part[4][0:2], 0, 1) + pad(part[1][1:2], 2, 0) + pad(up1[0:2], 1, 0),
        pad(part[4][2:4], 0, 1) + pad(part[7][2:3], 2, 0) + pad(down1[0:1], 0, 2) + pad(down1[1:2], 2, 0),
    )
    up, down = yield send(part[3][0:3] + pad(up2[0:2], 1, 0), part[5][1:4] + pad(down2[0:2], 0, 1))
    up, down = yield send(plus(part[2][1:4], up), plus(part[6][0:3], down))
    up, down = send(pad(part[1][2:4], 0, 1) + pad(up, 0, 0), pad(part[7][0:2], 1, 0) + pad(down, 0, 0))
    own = part[0]
    yield (
        pad(up, 2, 3) + pad(up1[2:3], 0, 7) + pad(up2[2:3], 1, 6)
        + pad(down, 5, 0) + pad(down2[2:3], 0, 7) + pad(down1[2:3], 1, 6)
        + pad(own[0:1], 7, 0) + pad(own[1:4], 0, 5)
    ).astype(bf16)


def call_options(rows, depth, columns):
    size = rows * depth + depth * columns + rows * columns
    return dict(
        compiler_params=pltpu.CompilerParams(vmem_limit_bytes=14 * 2**20),
        cost_estimate=pl.CostEstimate(
            flops=2 * rows * depth * columns, bytes_accessed=2 * size, transcendentals=0
        ),
    )


def dot(a, b, contract):
    return lax.dot_general(a, b, ((contract[:1], contract[1:]), ((), ())), preferred_element_type=jnp.float32)


def unproject_kernel(grad_ref, weight_ref, out_ref):
    total = jnp.dot(grad_ref[...], weight_ref[...], preferred_element_type=jnp.float32)
    out_ref[...] = total.astype(out_ref.dtype)


def unproject(grad, weight):
    rows, (hidden, features) = grad.shape[0], weight.shape
    tile = rows // 4
    return pl.pallas_call(
        unproject_kernel,
        grid=(4,),
        in_specs=[
            pl.BlockSpec((tile, hidden), lambda i: (i, 0)),
            pl.BlockSpec((hidden, features), lambda i: (0, 0)),
        ],
        out_specs=pl.BlockSpec((tile, features), lambda i: (i, 0)),
        out_shape=jax.ShapeDtypeStruct((rows, features), jnp.bfloat16),
        **call_options(rows, hidden, features),
    )(grad, weight)


FIRST_UP = (3, 6, 7)
FIRST_DOWN = (5, 2, 1)


def share_kernel(hid_ref, feat_ref, after_ref, out_ref, up_ref, down_ref, turned_ref):
    i = pl.program_id(0)

    @pl.when(i == 0)
    def _():
        turned_ref[...] = hid_ref[...].T

    total = jnp.dot(turned_ref[...], feat_ref[...], preferred_element_type=jnp.float32)
    total = total.astype(out_ref.dtype)
    out_ref[0] = total
    subset = total.shape[0] // 4
    for at in range(3):

        @pl.when(i == FIRST_UP[at])
        def _():
            up_ref[at] = total[:subset]

        @pl.when(i == FIRST_DOWN[at])
        def _():
            down_ref[at] = total[3 * subset :]


def weight_share(hid, feat, part, after):
    rows, hidden = hid.shape
    width = feat.shape[1] // (2 * NZ)
    first = pl.BlockSpec((3, hidden // 4, width), lambda i: (0, 0, 0))
    return pl.pallas_call(
        share_kernel,
        grid=(NZ,),
        in_specs=[
            pl.BlockSpec((rows, hidden), lambda i: (0, 0)),
            pl.BlockSpec((rows, width), lambda i: (0, part * NZ + i)),
            pl.BlockSpec(memory_space=pl.ANY),
        ],
        out_specs=[pl.BlockSpec((1, hidden, width), lambda i: (i, 0, 0)), first, first],
        out_shape=[
            jax.ShapeDtypeStruct(shape, jnp.bfloat16)
            for shape in [(NZ, hidden, width)] + [(3, hidden // 4, width)] * 2
        ],
        scratch_shapes=[pltpu.VMEM((hidden, rows), jnp.bfloat16)],
        **call_options(hidden, rows, NZ * width),
    )(hid, feat, after)


def per_device(tokens, out_grad, weight_in, weight_out):
    f32, bf16 = jnp.float32, jnp.bfloat16
    core = lax.axis_index("row") % NC
    z = lax.axis_index("col")
    n_tok, n_feat = tokens.shape
    half = n_feat // 2
    n_hid = weight_out.shape[0]
    sub = n_hid // 4

    def halves(value):
        return (
            lax.dynamic_slice_in_dim(value, core * half, half, axis=value.ndim - 1),
            lax.dynamic_slice_in_dim(value, (1 - core) * half, half, axis=value.ndim - 1),
        )

    with jax.named_scope("core_swap"):
        own, other = halves(jnp.stack([out_grad, tokens]))
        acts = jnp.stack(by_core(core, own, swap_core(other)), axis=1)
        acts, weight_in, weight_out = lax.optimization_barrier((acts, weight_in, weight_out))
        own, other = halves(jnp.stack([weight_in.T, weight_out]))
        low, high = by_core(core, own, swap_core(other))
        weights = jnp.concatenate([low.reshape(2, 4, sub, half), high.reshape(2, 4, sub, half)], axis=1)
        weights = rotate(weights.transpose(1, 0, 2, 3), (z + NZ - 2) % NZ, 11)
    block = n_tok // 4
    with jax.named_scope("tokens_over_z"):
        acts = acts.reshape(2, NC, 4, block, half).transpose(2, 0, 1, 3, 4)
        acts = lax.all_to_all(jnp.concatenate([acts, acts], axis=0), "col", 0, 0, tiled=True)
        acts = rotate(acts, z, NZ).reshape(NZ, 2, NC * block, half).transpose(1, 2, 0, 3)
        acts = acts.reshape(2, NC * block, NZ * half)
    with jax.named_scope("gather_tokens"):
        width = NZ * half
        acts = lax.all_gather(
            jnp.concatenate([acts[0], acts[1]], axis=1), "row", axis=0, tiled=True, axis_index_groups=CHIP_GROUPS
        )
    with jax.named_scope("spread_weights"):
        spread = spread_rest(weights, spread_first(weights))
        ring = next(spread)
        for step in range(3):
            ring = spread.send(lax.optimization_barrier(ring))
        w_in, w_out = spread.send(lax.optimization_barrier(ring))

    with jax.named_scope("projections"):
        pre_part = dot(acts[:, width:], w_in, (1, 1)).astype(bf16)
        pre = pre_part.astype(f32) + swap_core(pre_part).astype(f32)
        act_part = dot(acts[:, :width], w_out, (1, 1)).astype(bf16)
        act_grad = act_part.astype(f32) + swap_core(act_part).astype(f32)
        gelu_value, derivative = gelu_parts(pre)
        activated, derivative = lax.optimization_barrier((gelu_value.astype(bf16), derivative))
        pre_grad = (act_grad * derivative).astype(bf16)
    with jax.named_scope("tokens_grad_sum"):
        share = unproject(pre_grad, w_in)
        mark = swap_core(share[:16, :128])
        share = share.reshape(NY * NX, NC * block, width)
        share = lax.all_to_all(share, "row", 0, 0, tiled=True, axis_index_groups=CHIP_GROUPS)
    with jax.named_scope("weight_grads"):
        chains = [
            weight_grad_steps(*weight_share(activated, acts, 0, mark)),
            weight_grad_steps(*weight_share(pre_grad, acts, 1, mark)),
        ]
        moving = [next(c) for c in chains]
        for step in range(3):
            moving = [c.send(m) for c, m in zip(chains, moving)]
    with jax.named_scope("tokens_grad_sum"):
        share = jnp.sum(share.astype(f32), axis=0).astype(bf16)
        share = share.reshape(NC * block, NZ, half).transpose(1, 0, 2)
        share = rotate(share, (NZ - z) % NZ, NZ)
        share, moving[1] = lax.optimization_barrier((share, moving[1]))
        totals = [c.send(m) for c, m in zip(chains, moving)]

    with jax.named_scope("tokens_grad_home"):
        share = lax.all_to_all(share, "col", 0, 0, tiled=True).astype(f32)
        share = (share[0:4] + share[4:8]).reshape(4, NC, block, half).transpose(1, 0, 2, 3)
        share = share.reshape(NC, n_tok, half).astype(bf16)
        own = lax.dynamic_index_in_dim(share, core, axis=0, keepdims=False)
        other = lax.dynamic_index_in_dim(share, 1 - core, axis=0, keepdims=False)
        tokens_grad = jnp.concatenate(by_core(core, own, swap_core(other)), axis=1)

    with jax.named_scope("weight_grads_home"):
        grad_scale = float(n_tok * NY * NX * NC) ** (-0.5)
        grads = []
        for total in totals:
            total = jnp.concatenate([total, total[0:3]], axis=0)
            own, other = (
                lax.dynamic_slice_in_dim(total, (2 + NZ - z + 4 * c) % NZ, 4, axis=0).reshape(n_hid, half)
                for c in (core, 1 - core)
            )
            low, high = by_core(core, own, swap_core(other))
            grads.append(jnp.concatenate([low, high], axis=1).astype(f32) * grad_scale)
        weight_out_grad, weight_in_grad = grads[0], grads[1].T
    return (tokens_grad, weight_in_grad, weight_out_grad)


def solution(mesh):
    in_specs = (P("row", "col"), P("row", "col"), P("col", "row"), P("row", "col"))
    out_specs = (P("row", "col"), P("col", "row"), P("row", "col"))
    return jax.shard_map(
        per_device, mesh=mesh, in_specs=in_specs, out_specs=out_specs, check_vma=False
    )
```

```python
import math

import jax
import jax.numpy as jnp
from jax import lax
from jax.experimental import pallas as pl
from jax.experimental.pallas import tpu as pltpu
from jax.sharding import PartitionSpec as P

cubic_coeff = 0.044715
tanh_scale = math.sqrt(2.0 / math.pi)

NY, NX, NC, NZ = 4, 4, 2, 8
AXES = ("row", "col")


def gelu_parts(pre):
    inner = tanh_scale * (pre + cubic_coeff * pre * pre * pre)
    tangent = jnp.tanh(inner)
    gelu_value = 0.5 * pre * (1.0 + tangent)
    derivative = 0.5 * (1.0 + tangent) + 0.5 * pre * (1.0 - tangent * tangent) * tanh_scale * (
        1.0 + 3.0 * cubic_coeff * pre * pre
    )
    return (gelu_value, derivative)


def row_of(y, x, core):
    return ((y % NY) * NX + x % NX) * NC + core


def permute(value, target):
    pairs = [
        (row_of(y, x, c) * NZ + z, (lambda t: row_of(*t[:3]) * NZ + t[3] % NZ)(target(y, x, c, z)))
        for y in range(NY)
        for x in range(NX)
        for c in range(NC)
        for z in range(NZ)
    ]
    return lax.ppermute(value, AXES, pairs)


def swap_core(value):
    return permute(value, lambda y, x, c, z: (y, x, 1 - c, z))


def shift_z(value, step):
    return permute(value, lambda y, x, c, z: (y, x, c, z + step))


CHIP_GROUPS = [[row_of(y, x, c) for y in range(NY) for x in range(NX)] for c in range(NC)]


def by_core(core, own, other):
    first = core == 0
    return jnp.where(first, own, other), jnp.where(first, other, own)


def rotate(value, start, count):
    n = value.shape[0]
    copies = -(-(n - 1 + count) // n)
    long = jnp.concatenate([value] * copies, axis=0)
    return lax.dynamic_slice_in_dim(long, start, count, axis=0)


def cat(*values):
    return jnp.concatenate(values, axis=0)


def spread_first(local):
    return shift_z(local[2:5], 1), shift_z(local[5:8], -1)


def spread_rest(local, first):
    ups, downs = [first[0]], [first[1]]
    for step in range(2, 6):
        ups[-1], downs[-1] = yield ups[-1], downs[-1]
        up, down = ups[-1], downs[-1]
        if step == 4:
            up, down = cat(up[1:3], local[1:2]), cat(down[0:2], local[8:9])
        elif step == 5:
            up, down = cat(up[1:3], local[0:1]), cat(down[0:1], down[2:3], local[9:10])
        ups.append(shift_z(up, 1))
        downs.append(shift_z(down, -1))
    u1, u2, u3, u4, u5 = ups
    d1, d2, d3, d4, d5 = downs
    blocks = [
        (local[7:11],),
        (d1[1:3], d4[2:3], d5[2:3]),
        (d2, d5[1:2]),
        (u5[0:1], d3),
        (u4[0:2], d4[0:2]),
        (u3, d5[0:1]),
        (u5[1:2], u2),
        (u5[2:3], u4[2:3], u1[0:2]),
    ]
    hidden, feature = local.shape[2:]
    yield [
        jnp.concatenate([cat(*(p[:, i] for p in block)).reshape(4 * hidden, feature) for block in blocks], axis=1)
        for i in range(2)
    ]


def pad(value, before, after):
    return jnp.pad(value.astype(jnp.float32), ((before, after), (0, 0), (0, 0)))


def plus(a, b):
    return a.astype(jnp.float32) + b.astype(jnp.float32)


def weight_grad_steps(share, first_up, first_down):
    bf16 = jnp.bfloat16
    share = share.reshape(NZ, 4, share.shape[1] // 4, share.shape[2])
    part = [share[-k % NZ] for k in range(NZ)]
    send = lambda up, down: (shift_z(up.astype(bf16), -1), shift_z(down.astype(bf16), 1))
    up1, down1 = yield send(first_up, first_down)
    up2, down2 = yield send(
        pad(part[4][0:2], 0, 1) + pad(part[1][1:2], 2, 0) + pad(up1[0:2], 1, 0),
        pad(part[4][2:4], 0, 1) + pad(part[7][2:3], 2, 0) + pad(down1[0:1], 0, 2) + pad(down1[1:2], 2, 0),
    )
    up, down = yield send(part[3][0:3] + pad(up2[0:2], 1, 0), part[5][1:4] + pad(down2[0:2], 0, 1))
    up, down = yield send(plus(part[2][1:4], up), plus(part[6][0:3], down))
    up, down = send(pad(part[1][2:4], 0, 1) + pad(up, 0, 0), pad(part[7][0:2], 1, 0) + pad(down, 0, 0))
    own = part[0]
    yield (
        pad(up, 2, 3) + pad(up1[2:3], 0, 7) + pad(up2[2:3], 1, 6)
        + pad(down, 5, 0) + pad(down2[2:3], 0, 7) + pad(down1[2:3], 1, 6)
        + pad(own[0:1], 7, 0) + pad(own[1:4], 0, 5)
    ).astype(bf16)


def call_options(rows, depth, columns):
    size = rows * depth + depth * columns + rows * columns
    return dict(
        compiler_params=pltpu.CompilerParams(vmem_limit_bytes=14 * 2**20),
        cost_estimate=pl.CostEstimate(
            flops=2 * rows * depth * columns, bytes_accessed=2 * size, transcendentals=0
        ),
    )


def dot(a, b, contract):
    return lax.dot_general(a, b, ((contract[:1], contract[1:]), ((), ())), preferred_element_type=jnp.float32)


def unproject_kernel(grad_ref, weight_ref, out_ref):
    total = jnp.dot(grad_ref[...], weight_ref[...], preferred_element_type=jnp.float32)
    out_ref[...] = total.astype(out_ref.dtype)


def unproject(grad, weight):
    rows, (hidden, features) = grad.shape[0], weight.shape
    tile = rows // 4
    return pl.pallas_call(
        unproject_kernel,
        grid=(4,),
        in_specs=[
            pl.BlockSpec((tile, hidden), lambda i: (i, 0)),
            pl.BlockSpec((hidden, features), lambda i: (0, 0)),
        ],
        out_specs=pl.BlockSpec((tile, features), lambda i: (i, 0)),
        out_shape=jax.ShapeDtypeStruct((rows, features), jnp.bfloat16),
        **call_options(rows, hidden, features),
    )(grad, weight)


FIRST_UP = (3, 6, 7)
FIRST_DOWN = (5, 2, 1)


def share_kernel(hid_ref, feat_ref, after_ref, out_ref, up_ref, down_ref, turned_ref):
    i = pl.program_id(0)

    @pl.when(i == 0)
    def _():
        turned_ref[...] = hid_ref[...].T

    total = jnp.dot(turned_ref[...], feat_ref[...], preferred_element_type=jnp.float32)
    total = total.astype(out_ref.dtype)
    width = out_ref.shape[2]
    sides = total[:, :width], total[:, width:]
    out_ref[0], out_ref[1] = sides
    subset = total.shape[0] // 4
    for at in range(3):

        @pl.when(i == FIRST_UP[at] // 2)
        def _():
            up_ref[at] = sides[FIRST_UP[at] % 2][:subset]

        @pl.when(i == FIRST_DOWN[at] // 2)
        def _():
            down_ref[at] = sides[FIRST_DOWN[at] % 2][3 * subset :]


def weight_share(hid, feat, part, after):
    rows, hidden = hid.shape
    width = feat.shape[1] // (2 * NZ)
    first = pl.BlockSpec((3, hidden // 4, width), lambda i: (0, 0, 0))
    return pl.pallas_call(
        share_kernel,
        grid=(NZ // 2,),
        in_specs=[
            pl.BlockSpec((rows, hidden), lambda i: (0, 0)),
            pl.BlockSpec((rows, 2 * width), lambda i: (0, part * NZ // 2 + i)),
            pl.BlockSpec(memory_space=pl.ANY),
        ],
        out_specs=[pl.BlockSpec((2, hidden, width), lambda i: (i, 0, 0)), first, first],
        out_shape=[
            jax.ShapeDtypeStruct(shape, jnp.bfloat16)
            for shape in [(NZ, hidden, width)] + [(3, hidden // 4, width)] * 2
        ],
        scratch_shapes=[pltpu.VMEM((hidden, rows), jnp.bfloat16)],
        **call_options(hidden, rows, NZ * width),
    )(hid, feat, after)


def per_device(tokens, out_grad, weight_in, weight_out):
    f32, bf16 = jnp.float32, jnp.bfloat16
    core = lax.axis_index("row") % NC
    z = lax.axis_index("col")
    n_tok, n_feat = tokens.shape
    half = n_feat // 2
    n_hid = weight_out.shape[0]
    sub = n_hid // 4

    def halves(value):
        return (
            lax.dynamic_slice_in_dim(value, core * half, half, axis=value.ndim - 1),
            lax.dynamic_slice_in_dim(value, (1 - core) * half, half, axis=value.ndim - 1),
        )

    with jax.named_scope("core_swap"):
        own, other = halves(jnp.stack([out_grad, tokens]))
        acts = jnp.stack(by_core(core, own, swap_core(other)), axis=1)
        acts, weight_in, weight_out = lax.optimization_barrier((acts, weight_in, weight_out))
        own, other = halves(jnp.stack([weight_in.T, weight_out]))
        low, high = by_core(core, own, swap_core(other))
        weights = jnp.concatenate([low.reshape(2, 4, sub, half), high.reshape(2, 4, sub, half)], axis=1)
        weights = rotate(weights.transpose(1, 0, 2, 3), (z + NZ - 2) % NZ, 11)
    block = n_tok // 4
    with jax.named_scope("tokens_over_z"):
        acts = acts.reshape(2, NC, 4, block, half).transpose(2, 0, 1, 3, 4)
        acts = lax.all_to_all(jnp.concatenate([acts, acts], axis=0), "col", 0, 0, tiled=True)
        acts = rotate(acts, z, NZ).reshape(NZ, 2, NC * block, half).transpose(1, 2, 0, 3)
        acts = acts.reshape(2, NC * block, NZ * half)
    with jax.named_scope("gather_tokens"):
        width = NZ * half
        acts = lax.all_gather(
            jnp.concatenate([acts[0], acts[1]], axis=1), "row", axis=0, tiled=True, axis_index_groups=CHIP_GROUPS
        )
    with jax.named_scope("spread_weights"):
        spread = spread_rest(weights, spread_first(weights))
        ring = next(spread)
        for step in range(3):
            ring = spread.send(lax.optimization_barrier(ring))
        w_in, w_out = spread.send(lax.optimization_barrier(ring))

    with jax.named_scope("projections"):
        pre_part = dot(acts[:, width:], w_in, (1, 1)).astype(bf16)
        pre = pre_part.astype(f32) + swap_core(pre_part).astype(f32)
        act_part = dot(acts[:, :width], w_out, (1, 1)).astype(bf16)
        act_grad = act_part.astype(f32) + swap_core(act_part).astype(f32)
        gelu_value, derivative = gelu_parts(pre)
        activated, derivative = lax.optimization_barrier((gelu_value.astype(bf16), derivative))
        pre_grad = (act_grad * derivative).astype(bf16)
    with jax.named_scope("tokens_grad_sum"):
        share = unproject(pre_grad, w_in)
        mark = swap_core(share[:16, :128])
        share = share.reshape(NY * NX, NC * block, width)
        share = lax.all_to_all(share, "row", 0, 0, tiled=True, axis_index_groups=CHIP_GROUPS)
    with jax.named_scope("weight_grads"):
        chains = [
            weight_grad_steps(*weight_share(activated, acts, 0, mark)),
            weight_grad_steps(*weight_share(pre_grad, acts, 1, mark)),
        ]
        moving = [next(c) for c in chains]
        for step in range(3):
            moving = [c.send(m) for c, m in zip(chains, moving)]
    with jax.named_scope("tokens_grad_sum"):
        share = jnp.sum(share.astype(f32), axis=0).astype(bf16)
        share = share.reshape(NC * block, NZ, half).transpose(1, 0, 2)
        share = rotate(share, (NZ - z) % NZ, NZ)
        share, moving[1] = lax.optimization_barrier((share, moving[1]))
        totals = [c.send(m) for c, m in zip(chains, moving)]

    with jax.named_scope("tokens_grad_home"):
        share = lax.all_to_all(share, "col", 0, 0, tiled=True).astype(f32)
        share = (share[0:4] + share[4:8]).reshape(4, NC, block, half).transpose(1, 0, 2, 3)
        share = share.reshape(NC, n_tok, half).astype(bf16)
        own = lax.dynamic_index_in_dim(share, core, axis=0, keepdims=False)
        other = lax.dynamic_index_in_dim(share, 1 - core, axis=0, keepdims=False)
        tokens_grad = jnp.concatenate(by_core(core, own, swap_core(other)), axis=1)

    with jax.named_scope("weight_grads_home"):
        grad_scale = float(n_tok * NY * NX * NC) ** (-0.5)
        grads = []
        for total in totals:
            total = jnp.concatenate([total, total[0:3]], axis=0)
            own, other = (
                lax.dynamic_slice_in_dim(total, (2 + NZ - z + 4 * c) % NZ, 4, axis=0).reshape(n_hid, half)
                for c in (core, 1 - core)
            )
            low, high = by_core(core, own, swap_core(other))
            grads.append(jnp.concatenate([low, high], axis=1).astype(f32) * grad_scale)
        weight_out_grad, weight_in_grad = grads[0], grads[1].T
    return (tokens_grad, weight_in_grad, weight_out_grad)


def solution(mesh):
    in_specs = (P("row", "col"), P("row", "col"), P("col", "row"), P("row", "col"))
    out_specs = (P("row", "col"), P("col", "row"), P("row", "col"))
    return jax.shard_map(
        per_device, mesh=mesh, in_specs=in_specs, out_specs=out_specs, check_vma=False
    )
```

```python
import math

import jax
import jax.numpy as jnp
from jax import lax
from jax.experimental import pallas as pl
from jax.experimental.pallas import tpu as pltpu
from jax.sharding import PartitionSpec as P

cubic_coeff = 0.044715
tanh_scale = math.sqrt(2.0 / math.pi)

NY, NX, NC, NZ = 4, 4, 2, 8
AXES = ("row", "col")


def gelu_parts(pre):
    inner = tanh_scale * (pre + cubic_coeff * pre * pre * pre)
    tangent = jnp.tanh(inner)
    gelu_value = 0.5 * pre * (1.0 + tangent)
    derivative = 0.5 * (1.0 + tangent) + 0.5 * pre * (1.0 - tangent * tangent) * tanh_scale * (
        1.0 + 3.0 * cubic_coeff * pre * pre
    )
    return (gelu_value, derivative)


def row_of(y, x, core):
    return ((y % NY) * NX + x % NX) * NC + core


def permute(value, target):
    pairs = [
        (row_of(y, x, c) * NZ + z, (lambda t: row_of(*t[:3]) * NZ + t[3] % NZ)(target(y, x, c, z)))
        for y in range(NY)
        for x in range(NX)
        for c in range(NC)
        for z in range(NZ)
    ]
    return lax.ppermute(value, AXES, pairs)


def swap_core(value):
    return permute(value, lambda y, x, c, z: (y, x, 1 - c, z))


def shift_z(value, step):
    return permute(value, lambda y, x, c, z: (y, x, c, z + step))


CHIP_GROUPS = [[row_of(y, x, c) for y in range(NY) for x in range(NX)] for c in range(NC)]


def by_core(core, own, other):
    first = core == 0
    return jnp.where(first, own, other), jnp.where(first, other, own)


def rotate(value, start, count):
    n = value.shape[0]
    copies = -(-(n - 1 + count) // n)
    long = jnp.concatenate([value] * copies, axis=0)
    return lax.dynamic_slice_in_dim(long, start, count, axis=0)


def cat(*values):
    return jnp.concatenate(values, axis=0)


def spread_first(local):
    return shift_z(local[2:5], 1), shift_z(local[5:8], -1)


def spread_rest(local, first):
    ups, downs = [first[0]], [first[1]]
    for step in range(2, 6):
        ups[-1], downs[-1] = yield ups[-1], downs[-1]
        up, down = ups[-1], downs[-1]
        if step == 4:
            up, down = cat(up[1:3], local[1:2]), cat(down[0:2], local[8:9])
        elif step == 5:
            up, down = cat(up[1:3], local[0:1]), cat(down[0:1], down[2:3], local[9:10])
        ups.append(shift_z(up, 1))
        downs.append(shift_z(down, -1))
    u1, u2, u3, u4, u5 = ups
    d1, d2, d3, d4, d5 = downs
    blocks = [
        (local[7:11],),
        (d1[1:3], d4[2:3], d5[2:3]),
        (d2, d5[1:2]),
        (u5[0:1], d3),
        (u4[0:2], d4[0:2]),
        (u3, d5[0:1]),
        (u5[1:2], u2),
        (u5[2:3], u4[2:3], u1[0:2]),
    ]
    hidden, feature = local.shape[2:]
    yield [
        jnp.concatenate([cat(*(p[:, i] for p in block)).reshape(4 * hidden, feature) for block in blocks], axis=1)
        for i in range(2)
    ]


def pad(value, before, after):
    return jnp.pad(value.astype(jnp.float32), ((before, after), (0, 0), (0, 0)))


def plus(a, b):
    return a.astype(jnp.float32) + b.astype(jnp.float32)


def weight_grad_steps(share, first_up, first_down):
    bf16 = jnp.bfloat16
    share = share.reshape(NZ, 4, share.shape[1] // 4, share.shape[2])
    part = [share[-k % NZ] for k in range(NZ)]
    send = lambda up, down: (shift_z(up.astype(bf16), -1), shift_z(down.astype(bf16), 1))
    up1, down1 = yield send(first_up, first_down)
    up2, down2 = yield send(
        pad(part[4][0:2], 0, 1) + pad(part[1][1:2], 2, 0) + pad(up1[0:2], 1, 0),
        pad(part[4][2:4], 0, 1) + pad(part[7][2:3], 2, 0) + pad(down1[0:1], 0, 2) + pad(down1[1:2], 2, 0),
    )
    up, down = yield send(part[3][0:3] + pad(up2[0:2], 1, 0), part[5][1:4] + pad(down2[0:2], 0, 1))
    up, down = yield send(plus(part[2][1:4], up), plus(part[6][0:3], down))
    up, down = send(pad(part[1][2:4], 0, 1) + pad(up, 0, 0), pad(part[7][0:2], 1, 0) + pad(down, 0, 0))
    own = part[0]
    yield (
        pad(up, 2, 3) + pad(up1[2:3], 0, 7) + pad(up2[2:3], 1, 6)
        + pad(down, 5, 0) + pad(down2[2:3], 0, 7) + pad(down1[2:3], 1, 6)
        + pad(own[0:1], 7, 0) + pad(own[1:4], 0, 5)
    ).astype(bf16)


def call_options(rows, depth, columns):
    size = rows * depth + depth * columns + rows * columns
    return dict(
        compiler_params=pltpu.CompilerParams(vmem_limit_bytes=14 * 2**20),
        cost_estimate=pl.CostEstimate(
            flops=2 * rows * depth * columns, bytes_accessed=2 * size, transcendentals=0
        ),
    )


def dot(a, b, contract):
    return lax.dot_general(a, b, ((contract[:1], contract[1:]), ((), ())), preferred_element_type=jnp.float32)


def unproject_kernel(grad_ref, weight_ref, out_ref):
    total = jnp.dot(grad_ref[...], weight_ref[...], preferred_element_type=jnp.float32)
    out_ref[...] = total.astype(out_ref.dtype)


def unproject(grad, weight):
    rows, (hidden, features) = grad.shape[0], weight.shape
    tile = rows // 4
    return pl.pallas_call(
        unproject_kernel,
        grid=(4,),
        in_specs=[
            pl.BlockSpec((tile, hidden), lambda i: (i, 0)),
            pl.BlockSpec((hidden, features), lambda i: (0, 0)),
        ],
        out_specs=pl.BlockSpec((tile, features), lambda i: (i, 0)),
        out_shape=jax.ShapeDtypeStruct((rows, features), jnp.bfloat16),
        **call_options(rows, hidden, features),
    )(grad, weight)


FIRST_UP = (3, 6, 7)
FIRST_DOWN = (5, 2, 1)


def share_kernel(hid_ref, feat_ref, after_ref, out_ref, up_ref, down_ref, turned_ref):
    i = pl.program_id(0)

    @pl.when(i == 0)
    def _():
        turned_ref[...] = hid_ref[...].T

    total = jnp.dot(turned_ref[...], feat_ref[...], preferred_element_type=jnp.float32)
    total = total.astype(out_ref.dtype)
    width = out_ref.shape[2]
    sides = total[:, :width], total[:, width:]
    out_ref[0], out_ref[1] = sides
    subset = total.shape[0] // 4
    for at in range(3):

        @pl.when(i == FIRST_UP[at] // 2)
        def _():
            up_ref[at] = sides[FIRST_UP[at] % 2][:subset]

        @pl.when(i == FIRST_DOWN[at] // 2)
        def _():
            down_ref[at] = sides[FIRST_DOWN[at] % 2][3 * subset :]


def weight_share(hid, feat, part, after):
    rows, hidden = hid.shape
    width = feat.shape[1] // (2 * NZ)
    first = pl.BlockSpec((3, hidden // 4, width), lambda i: (0, 0, 0))
    return pl.pallas_call(
        share_kernel,
        grid=(NZ // 2,),
        in_specs=[
            pl.BlockSpec((rows, hidden), lambda i: (0, 0)),
            pl.BlockSpec((rows, 2 * width), lambda i: (0, part * NZ // 2 + i)),
            pl.BlockSpec(memory_space=pl.ANY),
        ],
        out_specs=[pl.BlockSpec((2, hidden, width), lambda i: (i, 0, 0)), first, first],
        out_shape=[
            jax.ShapeDtypeStruct(shape, jnp.bfloat16)
            for shape in [(NZ, hidden, width)] + [(3, hidden // 4, width)] * 2
        ],
        scratch_shapes=[pltpu.VMEM((hidden, rows), jnp.bfloat16)],
        **call_options(hidden, rows, NZ * width),
    )(hid, feat, after)


def hold_kernel(up_ref, down_ref, after_ref, up_out, down_out):
    up_out[...] = up_ref[...]
    down_out[...] = down_ref[...]


def hold(up, down, after):
    vmem = pl.BlockSpec(memory_space=pltpu.VMEM)
    return pl.pallas_call(
        hold_kernel,
        in_specs=[vmem, vmem, pl.BlockSpec(memory_space=pl.ANY)],
        out_specs=[vmem, vmem],
        out_shape=[jax.ShapeDtypeStruct(v.shape, v.dtype) for v in (up, down)],
    )(up, down, after)


def per_device(tokens, out_grad, weight_in, weight_out):
    f32, bf16 = jnp.float32, jnp.bfloat16
    core = lax.axis_index("row") % NC
    z = lax.axis_index("col")
    n_tok, n_feat = tokens.shape
    half = n_feat // 2
    n_hid = weight_out.shape[0]
    sub = n_hid // 4

    def halves(value):
        return (
            lax.dynamic_slice_in_dim(value, core * half, half, axis=value.ndim - 1),
            lax.dynamic_slice_in_dim(value, (1 - core) * half, half, axis=value.ndim - 1),
        )

    with jax.named_scope("core_swap"):
        own, other = halves(jnp.stack([out_grad, tokens]))
        acts = jnp.stack(by_core(core, own, swap_core(other)), axis=1)
        acts, weight_in, weight_out = lax.optimization_barrier((acts, weight_in, weight_out))
        own, other = halves(jnp.stack([weight_in.T, weight_out]))
        low, high = by_core(core, own, swap_core(other))
        weights = jnp.concatenate([low.reshape(2, 4, sub, half), high.reshape(2, 4, sub, half)], axis=1)
        weights = rotate(weights.transpose(1, 0, 2, 3), (z + NZ - 2) % NZ, 11)
    block = n_tok // 4
    with jax.named_scope("tokens_over_z"):
        acts = acts.reshape(2, NC, 4, block, half).transpose(2, 0, 1, 3, 4)
        acts = lax.all_to_all(jnp.concatenate([acts, acts], axis=0), "col", 0, 0, tiled=True)
        acts = rotate(acts, z, NZ).reshape(NZ, 2, NC * block, half).transpose(1, 2, 0, 3)
        acts = acts.reshape(2, NC * block, NZ * half)
    with jax.named_scope("gather_tokens"):
        width = NZ * half
        acts = lax.all_gather(
            jnp.concatenate([acts[0], acts[1]], axis=1), "row", axis=0, tiled=True, axis_index_groups=CHIP_GROUPS
        )
    with jax.named_scope("spread_weights"):
        spread = spread_rest(weights, spread_first(weights))
        ring = next(spread)
        for step in range(3):
            ring = spread.send(lax.optimization_barrier(ring))
        w_in, w_out = spread.send(lax.optimization_barrier(ring))

    with jax.named_scope("projections"):
        pre_part = dot(acts[:, width:], w_in, (1, 1)).astype(bf16)
        pre = pre_part.astype(f32) + swap_core(pre_part).astype(f32)
        act_part = dot(acts[:, :width], w_out, (1, 1)).astype(bf16)
        act_grad = act_part.astype(f32) + swap_core(act_part).astype(f32)
        gelu_value, derivative = gelu_parts(pre)
        activated, derivative = lax.optimization_barrier((gelu_value.astype(bf16), derivative))
        pre_grad = (act_grad * derivative).astype(bf16)
    with jax.named_scope("tokens_grad_sum"):
        share = unproject(pre_grad, w_in)
        mark = swap_core(share[:16, :128])
        share = share.reshape(NY * NX, NC * block, width)
        share = lax.all_to_all(share, "row", 0, 0, tiled=True, axis_index_groups=CHIP_GROUPS)
    with jax.named_scope("weight_grads"):
        chains = [
            weight_grad_steps(*weight_share(activated, acts, 0, mark)),
            weight_grad_steps(*weight_share(pre_grad, acts, 1, mark)),
        ]
        moving = [next(c) for c in chains]
        for step in range(3):
            moving = [c.send(m) for c, m in zip(chains, moving)]
    with jax.named_scope("tokens_grad_sum"):
        share = jnp.sum(share.astype(f32), axis=0).astype(bf16)
        share = share.reshape(NC * block, NZ, half).transpose(1, 0, 2)
        share = rotate(share, (NZ - z) % NZ, NZ)
        moving[1] = hold(*moving[1], swap_core(share[0, :16, :128]))
        totals = [c.send(m) for c, m in zip(chains, moving)]

    with jax.named_scope("tokens_grad_home"):
        share = lax.all_to_all(share, "col", 0, 0, tiled=True).astype(f32)
        share = (share[0:4] + share[4:8]).reshape(4, NC, block, half).transpose(1, 0, 2, 3)
        share = share.reshape(NC, n_tok, half).astype(bf16)
        own = lax.dynamic_index_in_dim(share, core, axis=0, keepdims=False)
        other = lax.dynamic_index_in_dim(share, 1 - core, axis=0, keepdims=False)
        tokens_grad = jnp.concatenate(by_core(core, own, swap_core(other)), axis=1)

    with jax.named_scope("weight_grads_home"):
        grad_scale = float(n_tok * NY * NX * NC) ** (-0.5)
        grads = []
        for total in totals:
            total = jnp.concatenate([total, total[0:3]], axis=0)
            own, other = (
                lax.dynamic_slice_in_dim(total, (2 + NZ - z + 4 * c) % NZ, 4, axis=0).reshape(n_hid, half)
                for c in (core, 1 - core)
            )
            low, high = by_core(core, own, swap_core(other))
            grads.append(jnp.concatenate([low, high], axis=1).astype(f32) * grad_scale)
        weight_out_grad, weight_in_grad = grads[0], grads[1].T
    return (tokens_grad, weight_in_grad, weight_out_grad)


def solution(mesh):
    in_specs = (P("row", "col"), P("row", "col"), P("col", "row"), P("row", "col"))
    out_specs = (P("row", "col"), P("col", "row"), P("row", "col"))
    return jax.shard_map(
        per_device, mesh=mesh, in_specs=in_specs, out_specs=out_specs, check_vma=False
    )
```
